32 devices in a mesh: dp: 4 (over z), seq: 8 (over y, x, core).
Axes of the slice: x: 2, y: 2, z: 4, core: 2. Of those that a mesh axis runs over, the one named last changes fastest.
Arguments:
- queries: bfloat16 [12288, 2048], P(('dp', 'seq')), parts along dimension 0, may hold values from -6 to 6
- keys_in: bfloat16 [12288, 2048], P(('dp', 'seq')), parts along dimension 0, may hold values from -6 to 6
- values: bfloat16 [12288, 2048], P(('dp', 'seq')), parts along dimension 0, may hold values from -6 to 6
- stream: bfloat16 [12288, 2048], P(('dp', 'seq')), parts along dimension 0, may hold values from -6 to 6
- log_decay: float32 [12288, 16], P(('dp', 'seq')), parts along dimension 0, may hold values from -1 to 0
- token_index: int32 [32, 768], P('dp', 'seq'), parts along dimension 0, may hold values from 0 to 3071, as said below
- route_weight: float32 [32, 768], P('dp', 'seq'), parts along dimension 0, may hold values from 0.2 to 1
- moe_gain: float32 [2048], replicated, may hold values from 0.25 to 1.75
- out_weight: bfloat16 [2048, 2048], P('seq'), may hold values from -0.125 to 0.125
- gate_weight: bfloat16 [8, 2048, 1408], P('seq'), may hold values from -0.125 to 0.125
- up_weight: bfloat16 [8, 2048, 1408], P('seq'), may hold values from -0.125 to 0.125
- down_weight: bfloat16 [8, 1408, 2048], P('seq'), may hold values from -0.15625 to 0.15625
Outputs:
- mixed: bfloat16 [12288, 2048], P(('dp', 'seq')), parts along dimension 0
The draws below stay inside these ranges and needn't reach their ends.
There are 4 independent parts, one for each index of `dp`. The reference program is written for one: setup_inputs(seed, part) draws one part's arguments, and reference() takes and returns one part's arrays. A program takes and returns all parts, laid end to end along the dimension named above; an argument that names none is the same for every part. Nothing has to cross between parts.
Inputs may be any that keep to these rules, and one draw needn't show every extreme that they name: `token_index`: for each expert and each j, positions j * 96 to (j + 1) * 96 - 1 of its row hold 96 different tokens of the j-th block of 384 tokens, in ascending order.
All inputs are finite; a program needn't handle non-finite values.
Results may differ from the reference program's by a relative error of at most 0.014.
Values may be sent and summed in bfloat16 or wider, within the bound.
A program may use at most 192 MiB of HBM per device.

```python
import math
import jax
import jax.numpy as jnp
from jax import lax

D = 2048
H = 16
DH = 128
FF = 1408
TOK_DEV = 384
SPAN_TOKENS = 3072
EXPERTS = 8
CAP = 768
PER_SRC = 96


def draw_log_decay(key, part):
    segment_parts = jax.random.split(key, 9)
    blocks = SPAN_TOKENS // TOK_DEV
    forget_count = max(1, H // 2)
    ranking = jax.random.permutation(segment_parts[0], H)
    forgetting = ranking < forget_count
    block_strength = jnp.exp(jax.random.uniform(segment_parts[1], (blocks, H), minval=math.log(0.2), maxval=math.log(12.0))) / TOK_DEV
    keep_rate = jnp.exp(jax.random.uniform(segment_parts[2], (H,), minval=math.log(0.02), maxval=math.log(0.1))) / SPAN_TOKENS
    keep_factor = jnp.exp(jax.random.uniform(segment_parts[3], (blocks, H), minval=math.log(0.6), maxval=math.log(1.8)))
    raised_block = jax.random.randint(segment_parts[4], (H,), 0, blocks)
    raised_amount = jnp.exp(jax.random.uniform(segment_parts[5], (H,), minval=math.log(0.35), maxval=math.log(0.6))) / TOK_DEV
    block_numbers = jnp.arange(blocks)
    keep_strength = keep_rate[None, :] * keep_factor + jnp.where(block_numbers[:, None] == raised_block[None, :], raised_amount[None, :], 0.0)
    strength = jnp.where(forgetting[None, :], block_strength, keep_strength)
    position_factor = jax.random.uniform(segment_parts[6], (SPAN_TOKENS, H), minval=0.5, maxval=1.5)
    token_values = jnp.minimum(jnp.repeat(strength, TOK_DEV, axis=0) * position_factor, 0.3)
    segment_start = jax.random.randint(segment_parts[7], (2,), 0, SPAN_TOKENS)
    segment_length = jax.random.uniform(segment_parts[8], (2,), minval=math.log(0.5), maxval=math.log(0.8))
    token_places = jnp.arange(SPAN_TOKENS)
    segment_list = jnp.where(token_places == segment_start[0], segment_length[0], 0.0) + jnp.where(token_places == segment_start[1], segment_length[1], 0.0)
    combined_output = -token_values + segment_list[:, None]
    return combined_output.astype(jnp.float32)


def draw_token_index(key, part):
    sources = SPAN_TOKENS // TOK_DEV
    streams = jax.random.split(key, EXPERTS * sources)
    shuffled = jax.vmap(lambda single: jax.random.permutation(single, TOK_DEV))(streams)
    chosen = jnp.sort(shuffled[:, :PER_SRC], axis=1).reshape(EXPERTS, sources, PER_SRC)
    chosen = chosen + (jnp.arange(sources) * TOK_DEV)[None, :, None]
    return chosen.reshape(EXPERTS, CAP).astype(jnp.int32)


def block_scale(own_key, dims, shards, least, largest):
    level, own = 1.0, jax.random.fold_in(own_key, 6)
    for position, shards_of in shards:
        steps = jnp.exp(jax.random.uniform(jax.random.fold_in(own, position), (shards_of,), jnp.float32, least / len(shards), largest / len(shards)))
        level = level * jnp.repeat(steps, dims[position] // shards_of).reshape([-1 if axis == position else 1 for axis in range(len(dims))])
    return level


def normal_values(rng, shape, scale, bound, cuts=(), dtype=jnp.bfloat16):
    entries = scale * jax.random.normal(rng, shape, jnp.float32)
    if cuts:
        entries = entries * block_scale(rng, shape, cuts, -0.22, 0.18)
    return jnp.clip(entries, -bound, bound).astype(dtype)


def setup_inputs(seed: int = 0, part: int = 0) -> dict:
    seeds = jax.random.split(jax.random.key(seed), 13)
    part_keys = jax.random.split(jax.random.fold_in(seeds[12], part), 13)
    queries = normal_values(part_keys[0], (SPAN_TOKENS, D), 1.0, 6.0, ((0, 8),))
    keys_in = normal_values(part_keys[1], (SPAN_TOKENS, D), 1.0, 6.0, ((0, 8),))
    values = normal_values(part_keys[2], (SPAN_TOKENS, D), 1.0, 6.0, ((0, 8),))
    stream = normal_values(part_keys[3], (SPAN_TOKENS, D), 1.0, 6.0, ((0, 8),))
    log_decay = draw_log_decay(jax.random.fold_in(jax.random.fold_in(seeds[12], part), 71), part)
    token_index = draw_token_index(jax.random.fold_in(jax.random.fold_in(seeds[12], part), 71), part)
    route_weight = jnp.clip(0.2 + 0.8 * jax.random.uniform(part_keys[6], (EXPERTS, CAP), jnp.float32) ** block_scale(part_keys[6], (EXPERTS, CAP), ((1, 8),), -0.2, 0.2), 0.2, 1.0)
    moe_gain = jnp.clip(1.0 + 0.15 * jax.random.normal(seeds[7], (D,), jnp.float32), 0.25, 1.75)
    out_weight = normal_values(seeds[8], (D, D), D ** -0.5, 0.125, ((0, 8),))
    gate_weight = normal_values(seeds[9], (EXPERTS, D, FF), D ** -0.5, 0.125, ((0, 8),))
    up_weight = normal_values(seeds[10], (EXPERTS, D, FF), D ** -0.5, 0.125, ((0, 8),))
    down_weight = normal_values(seeds[11], (EXPERTS, FF, D), FF ** -0.5, 0.15625, ((0, 8),))
    return {"queries": queries, "keys_in": keys_in, "values": values, "stream": stream, "log_decay": log_decay, "token_index": token_index, "route_weight": route_weight, "moe_gain": moe_gain, "out_weight": out_weight, "gate_weight": gate_weight, "up_weight": up_weight, "down_weight": down_weight}


def reference(queries, keys_in, values, stream, log_decay, token_index, route_weight, moe_gain, out_weight, gate_weight, up_weight, down_weight):
    blocks = SPAN_TOKENS // TOK_DEV
    scaling = DH ** (-0.5)
    highest = lax.Precision.HIGHEST
    query_blocks = queries.reshape(blocks, TOK_DEV, H, DH)
    key_blocks = keys_in.reshape(blocks, TOK_DEV, H, DH)
    value_blocks = values.reshape(blocks, TOK_DEV, H, DH)
    decay_blocks = log_decay.reshape(blocks, TOK_DEV, H)
    causal = jnp.arange(TOK_DEV)[:, None] >= jnp.arange(TOK_DEV)[None, :]

    def one_block(carried, inputs):
        query_part, key_part, value_part, decay_part = inputs
        running = jnp.cumsum(decay_part, axis=0)
        ending = running[-1]
        spacing = running[:, None, :] - running[None, :, :]
        decay_mask = jnp.where(causal[:, :, None], jnp.exp(jnp.minimum(spacing, 0.0)), 0.0)
        query_wide = query_part.astype(jnp.float32)
        key_wide = key_part.astype(jnp.float32)
        value_wide = value_part.astype(jnp.float32)
        scores = (jnp.einsum('thd,shd->tsh', query_wide, key_wide, precision=highest) * scaling * decay_mask).astype(jnp.bfloat16)
        within = jnp.einsum('tsh,shd->thd', lax.optimization_barrier(scores).astype(jnp.float32), value_wide, precision=highest)
        query_scaled = (query_wide * (jnp.exp(running) * scaling)[:, :, None]).astype(jnp.bfloat16)
        state_low = carried.astype(jnp.bfloat16)
        across = jnp.einsum('thd,hde->the', lax.optimization_barrier(query_scaled).astype(jnp.float32), lax.optimization_barrier(state_low).astype(jnp.float32), precision=highest)
        key_scaled = (key_wide * jnp.exp(ending[None, :] - running)[:, :, None]).astype(jnp.bfloat16)
        local_state = jnp.einsum('shd,she->hde', lax.optimization_barrier(key_scaled).astype(jnp.float32), value_wide, precision=highest)
        following = carried * jnp.exp(ending)[:, None, None] + local_state
        return (following, within + across)
    initial = jnp.zeros((H, DH, DH), jnp.float32)
    _, attention = lax.scan(one_block, initial, (query_blocks, key_blocks, value_blocks, decay_blocks))
    attention = attention.reshape(SPAN_TOKENS, H, DH)
    spread = lax.optimization_barrier(jnp.mean(attention * attention, axis=2, keepdims=True))
    normed = (attention * lax.rsqrt(spread + 1e-06)).astype(jnp.bfloat16).reshape(SPAN_TOKENS, D)
    attended = jnp.dot(normed, out_weight, preferred_element_type=jnp.float32)
    residual = (stream.astype(jnp.float32) + attended).astype(jnp.bfloat16)
    widened = residual.astype(jnp.float32)
    mixed_in = (widened * lax.rsqrt(lax.optimization_barrier(jnp.mean(widened * widened, axis=1, keepdims=True)) + 1e-06) * moe_gain).astype(jnp.bfloat16)

    def one_expert(inputs):
        chosen, gating_w, upward_w, downward_w = inputs
        picked = jnp.take(mixed_in, chosen, axis=0).astype(jnp.float32)
        gating = jnp.dot(picked, gating_w.astype(jnp.float32), precision=highest)
        upward = jnp.dot(picked, upward_w.astype(jnp.float32), precision=highest)
        activated = (jax.nn.silu(gating) * upward).astype(jnp.bfloat16)
        product = jnp.dot(lax.optimization_barrier(activated).astype(jnp.float32), downward_w.astype(jnp.float32), precision=highest)
        return product.astype(jnp.bfloat16)
    expert_out = lax.map(one_expert, (token_index, gate_weight, up_weight, down_weight))
    weighted = expert_out.astype(jnp.float32) * route_weight[:, :, None]
    total = widened.at[token_index.reshape(-1)].add(weighted.reshape(-1, D))
    return total.astype(jnp.bfloat16)
```

```python
import functools

import jax
import jax.numpy as jnp
from jax import lax
from jax.experimental import pallas as pl
from jax.experimental.pallas import tpu as pltpu
from jax.sharding import PartitionSpec as P

MESH = pl.DeviceIdType.MESH
F32, BF16 = jnp.float32, jnp.bfloat16
EXACT = lax.Precision.HIGHEST


def flipped(index, offset):
    bit = 1
    while bit <= offset:
        if offset & bit:
            index = index + bit * (1 - 2 * ((index // bit) % 2))
        bit *= 2
    return index


def remote(src, dst, send, recv, peer):
    return pltpu.make_async_remote_copy(
        src_ref=src, dst_ref=dst, send_sem=send, recv_sem=recv,
        device_id={"seq": peer}, device_id_type=MESH,
    )


def greet(n, me):
    barrier = pltpu.get_barrier_semaphore()
    for offset in range(1, n):
        pl.semaphore_signal(
            barrier, inc=1, device_id={"seq": flipped(me, offset)}, device_id_type=MESH
        )
    pl.semaphore_wait(barrier, n - 1)


def attend_kernel(
    n, heads, size,
    q_h, k_h, v_h, s_h, ld, ldt, gain, w_h,
    res, mix,
    q, k, v, stream, weight, att, normed, run, runt,
    state, state_low, state_mate, total, before, give, take, before_low, before_mate,
    incoming, ends, coef,
    load_sem, w_send, w_recv, e_send, e_recv, s_send, s_recv,
):
    me = lax.axis_index("seq")
    core, chip = me % 2, me // 2
    mate = flipped(me, 1)
    length, width = q.shape
    rows = w_h.shape[0]
    half = heads // 2
    low = rows // 2
    bits = n.bit_length() - 2
    scaling = size ** (-0.5)

    loads = [
        pltpu.make_async_copy(src, dst, load_sem.at[i])
        for i, (src, dst) in enumerate(((k_h, k), (v_h, v), (q_h, q), (s_h, stream)))
    ]
    own_rows = pl.ds(pl.multiple_of(me * rows, rows), rows)
    loads.append(pltpu.make_async_copy(w_h, weight.at[own_rows], load_sem.at[4]))
    for copy in loads:
        copy.start()
    greet(n, me)

    def part(offset, piece):
        start = flipped(me, offset) * rows
        if piece == 0:
            return pl.ds(pl.multiple_of(start, low), low)
        if piece == 1:
            return pl.ds(pl.multiple_of(start + low, low), low)
        return pl.ds(pl.multiple_of(start, rows), rows)

    def own(piece):
        return w_h.at[pl.ds(piece * low, low)] if piece < 2 else w_h

    def spread(slot, src, where, offset):
        return remote(src, weight.at[where], w_send.at[slot], w_recv.at[slot], flipped(me, offset))

    square = n == 8
    if square:
        first = [
            spread(0, own(0), part(0, 0), 2),
            spread(1, own(1), part(0, 1), 4),
        ]
        second = [
            spread(2, own(1), part(0, 1), 2),
            spread(3, own(0), part(0, 0), 4),
        ]
        onward = [
            spread(4, weight.at[part(2, 0)], part(2, 0), 4),
            spread(5, weight.at[part(4, 1)], part(4, 1), 2),
        ]
        across_own = [spread(6, own(2), part(0, 2), 1)]
        across = [
            spread(7 + i, weight.at[part(o, p)], part(o, p), 1)
            for i, (o, p) in enumerate(((2, 0), (4, 1), (2, 1), (4, 0), (6, 0), (6, 1)))
        ]
    else:
        others = range(2, n, 2)
        first = [spread(o, own(2), part(0, 2), o) for o in others]
        second, onward = [], []
        across_own = [spread(1, own(2), part(0, 2), 1)]
        across = [spread(o + 1, weight.at[part(o, 2)], part(o, 2), 1) for o in others]
    for copy in first + across_own:
        copy.start()

    wide = lax.broadcasted_iota(jnp.int32, (length, length), 0)
    tall = lax.broadcasted_iota(jnp.int32, (length, length), 1)
    lower = (wide >= tall).astype(F32)
    upper = (wide <= tall).astype(F32)
    run[...] = jnp.dot(lower, ld[...], precision=EXACT, preferred_element_type=F32)
    runt[...] = jnp.dot(ldt[...], upper, precision=EXACT, preferred_element_type=F32)
    ends[me] = jnp.dot(
        ldt[...], jnp.ones((length, size), F32), precision=EXACT, preferred_element_type=F32
    )
    tell = [
        remote(ends.at[me], ends.at[me], e_send.at[o], e_recv.at[o], flipped(me, o))
        for o in range(1, n)
    ]
    for copy in tell:
        copy.start()

    def column(h, lanes):
        pick = (lax.broadcasted_iota(jnp.int32, (heads, lanes), 0) == h).astype(F32)
        return jnp.dot(run[...], pick, precision=EXACT, preferred_element_type=F32)

    def lanes_of(h):
        return pl.ds(pl.multiple_of(h * size, size), size)

    loads[0].wait()
    loads[1].wait()

    @pl.loop(0, heads)
    def _(h):
        shrink = jnp.exp(ends[me, pl.ds(h, 1), :] - column(h, size))
        scaled = (k[:, lanes_of(h)].astype(F32) * shrink).astype(BF16)
        new = lax.dot_general(
            scaled, v[:, lanes_of(h)], (((0,), (0,)), ((), ())), preferred_element_type=F32
        )
        state[h] = new
        state_low[h] = new.astype(BF16)

    swap = remote(state_low, state_mate, s_send.at[0], s_recv.at[0], mate)
    swap.start()
    for copy in tell:
        copy.wait()
    swap.wait()

    first_end, last_end = ends[2 * chip], ends[2 * chip + 1]
    coef[0] = jnp.exp(last_end)

    @pl.loop(0, half)
    def _(j):
        h = core * half + j
        mine, theirs = state[h], state_mate[h].astype(F32)
        early = jnp.where(core == 0, mine, theirs)
        late = jnp.where(core == 0, theirs, mine)
        both = early * coef[0, pl.ds(h, 1), :] + late
        total[j] = both
        give[0, j] = both.astype(BF16)
        before[j] = jnp.zeros_like(both)

    def exchange(b):
        return remote(
            give.at[b], take.at[b], s_send.at[b + 1], s_recv.at[b + 1], flipped(me, 2 << b)
        )

    def bit_of(b):
        return (me // (2 << b)) % 2

    def send_state(b):
        if b < bits - 1:
            exchange(b).start()
        else:

            @pl.when(bit_of(b) == 0)
            def _():
                exchange(b).start()

    send_state(0)
    for copy in second:
        copy.start()
    loads[2].wait()

    def attend(h):
        weights = lax.dot_general(
            q[:, lanes_of(h)], k[:, lanes_of(h)], (((1,), (1,)), ((), ())),
            preferred_element_type=F32,
        ) * scaling
        spacing = column(h, length) - runt[pl.ds(h, 1), :]
        decay = jnp.where(wide >= tall, jnp.exp(jnp.minimum(spacing, 0.0)), 0.0)
        att[:, lanes_of(h)] = jnp.dot(
            (weights * decay).astype(BF16), v[:, lanes_of(h)], preferred_element_type=F32
        )

    pl.loop(0, heads)(attend)

    group, ahead = first_end + last_end, jnp.zeros_like(first_end)
    for b in range(bits):
        base = (flipped(me, 2 << b) // (2 << b)) * (2 << b)
        other = ends[base]
        for i in range(1, 2 << b):
            other = other + ends[base + i]
        bit = bit_of(b)
        coef[0] = jnp.exp(ahead)
        coef[1] = jnp.where(bit == 1, jnp.exp(group), 1.0)
        coef[2] = jnp.where(bit == 1, 1.0, jnp.exp(other))
        if b < bits - 1:
            exchange(b).wait()
        else:

            @pl.when(bit == 0)
            def _():
                exchange(b).wait_send()

            @pl.when(bit == 1)
            def _():
                exchange(b).wait_recv()

        @pl.when(bit == 1)
        def _():
            @pl.loop(0, half)
            def _(j):
                h = core * half + j
                before[j] += take[b, j].astype(F32) * coef[0, pl.ds(h, 1), :]

        if b < bits - 1:

            @pl.loop(0, half)
            def _(j):
                h = core * half + j
                both = (
                    take[b, j].astype(F32) * coef[1, pl.ds(h, 1), :]
                    + total[j] * coef[2, pl.ds(h, 1), :]
                )
                total[j] = both
                give[b + 1, j] = both.astype(BF16)

            send_state(b + 1)
        ahead = ahead + jnp.where(bit == 1, other, 0.0)
        group = group + other
        if b == 0 and square:
            first[0].wait_recv()
            onward[0].start()
            across[0].start()
            first[1].wait_recv()
            onward[1].start()
            across[1].start()

    before_low[...] = before[...].astype(BF16)
    trade = remote(before_low, before_mate, s_send.at[bits + 1], s_recv.at[bits + 1], mate)
    trade.start()
    trade.wait()
    coef[0] = jnp.where(core == 1, jnp.exp(first_end), 1.0)

    @pl.loop(0, half)
    def _(j):
        for h, earlier in (
            (core * half + j, before[j]),
            ((1 - core) * half + j, before_mate[j].astype(F32)),
        ):
            mate_part = jnp.where(core == 1, state_mate[h].astype(F32), 0.0)
            incoming[h] = (earlier * coef[0, pl.ds(h, 1), :] + mate_part).astype(BF16)

    @pl.loop(0, heads)
    def _(h):
        grown = jnp.exp(column(h, size)) * scaling
        scaled = (q[:, lanes_of(h)].astype(F32) * grown).astype(BF16)
        whole = att[:, lanes_of(h)] + jnp.dot(scaled, incoming[h], preferred_element_type=F32)
        mean = jnp.mean(whole * whole, axis=1, keepdims=True)
        normed[:, lanes_of(h)] = (whole * lax.rsqrt(mean + 1e-06)).astype(BF16)

    tile = 512

    def project(offset, fresh):
        start = (flipped(me, offset) // 2) * (2 * rows)
        inner = pl.ds(pl.multiple_of(start, 2 * rows), 2 * rows)

        @pl.loop(0, width // tile)
        def _(i):
            cols = pl.ds(pl.multiple_of(i * tile, tile), tile)
            term = jnp.dot(normed[:, inner], weight[inner, cols], preferred_element_type=F32)
            att[:, cols] = term if fresh else att[:, cols] + term

    loads[4].wait()
    across_own[0].wait()
    project(0, True)
    if square:
        second[0].wait_recv()
        across[2].start()
        second[1].wait_recv()
        across[3].start()
        across[0].wait()
        across[2].wait()
        project(2, False)
        across[1].wait()
        across[3].wait()
        project(4, False)
        onward[0].wait_recv()
        across[4].start()
        onward[1].wait_recv()
        across[5].start()
        loads[3].wait()
        across[4].wait()
        across[5].wait()
        project(6, False)
        for copy in first + second + onward:
            copy.wait_send()
    else:
        for i, copy in enumerate(first):
            copy.wait()
            across[i].start()
        loads[3].wait()
        for i, offset in enumerate(range(2, n, 2)):
            across[i].wait()
            project(offset, False)

    step = 64

    @pl.loop(0, length // step)
    def _(i):
        at = pl.ds(pl.multiple_of(i * step, step), step)
        kept = (stream[at, :].astype(F32) + att[at, :]).astype(BF16)
        res[at, :] = kept
        kept = kept.astype(F32)
        mean = jnp.mean(kept * kept, axis=1, keepdims=True)
        mix[at, :] = (kept * lax.rsqrt(mean + 1e-06) * gain[...]).astype(BF16)


def expert_kernel(
    n, slots,
    mix, res, tok_col, tok_row, route, gate_h, up_h, down_h,
    out,
    gate, up, down, picked, arrived, hidden, produced, returned,
    load_sem, a_send, a_recv, b_send, b_recv,
):
    me = lax.axis_index("seq")
    length, width = mix.shape
    inner = gate.shape[1]
    loads = [
        pltpu.make_async_copy(src, dst, load_sem.at[i])
        for i, (src, dst) in enumerate(((gate_h, gate), (up_h, up), (down_h, down)))
    ]
    for copy in loads:
        copy.start()
    greet(n, me)

    def block(first, count=1):
        return pl.ds(first * slots, count * slots)

    def pick(first, count, into):
        lines = block(first, count)
        places = lax.broadcasted_iota(jnp.int32, (count * slots, length), 1)
        chosen = (tok_col[lines, :] == places).astype(F32).astype(BF16)
        tile = 512

        @pl.loop(0, width // tile)
        def _(i):
            cols = pl.ds(pl.multiple_of(i * tile, tile), tile)
            into[lines, cols] = jnp.dot(
                chosen, mix[:, cols], preferred_element_type=F32
            ).astype(BF16)

    def out_copy(o):
        return remote(
            picked.at[block(o)], arrived.at[block(o)], a_send.at[o], a_recv.at[o], flipped(me, o)
        )

    def back_copy(o):
        return remote(
            produced.at[block(o)], returned.at[block(o)], b_send.at[o], b_recv.at[o],
            flipped(me, o),
        )

    def expert(first, count):
        lines = block(first, count)
        tile = 256

        def upward(cols):
            x = arrived[lines, :]
            a = jnp.dot(x, gate[:, cols], preferred_element_type=F32)
            b = jnp.dot(x, up[:, cols], preferred_element_type=F32)
            hidden[lines, cols] = (a / (1.0 + jnp.exp(-a)) * b).astype(BF16)

        @pl.loop(0, inner // tile)
        def _(i):
            upward(pl.ds(pl.multiple_of(i * tile, tile), tile))

        if inner % tile:
            upward(pl.ds(inner - inner % tile, inner % tile))

        wide = 512

        @pl.loop(0, width // wide)
        def _(i):
            cols = pl.ds(pl.multiple_of(i * wide, wide), wide)
            produced[lines, cols] = jnp.dot(
                hidden[lines, :], down[:, cols], preferred_element_type=F32
            ).astype(BF16)

    near = list(range(2, n - n // 4))
    far = list(range(n - n // 4, n))
    pick(2, len(near), picked)
    for o in near:
        out_copy(o).start()
    pick(1, 1, picked)
    out_copy(1).start()
    pick(0, 1, arrived)
    pick(far[0], len(far), picked)
    for copy in loads:
        copy.wait()
    out_copy(1).wait()
    expert(0, 2)
    back_copy(1).start()
    returned[block(0), :] = produced[block(0), :]
    for o in near:
        out_copy(o).wait_send()
    for o in far:
        out_copy(o).start()
    for o in near:
        out_copy(o).wait_recv()
    expert(2, len(near))
    for o in near:
        back_copy(o).start()
    for o in far:
        out_copy(o).wait()
    expert(far[0], len(far))
    for o in far:
        back_copy(o).start()

    for o in range(1, n):
        back_copy(o).wait()
    lines = lax.broadcasted_iota(jnp.int32, (length, n * slots), 0)
    mixing = jnp.where(tok_row[...] == lines, route[...], 0.0).astype(BF16)
    tile = 512

    @pl.loop(0, width // tile)
    def _(i):
        cols = pl.ds(pl.multiple_of(i * tile, tile), tile)
        gathered = jnp.dot(mixing, returned[:, cols], preferred_element_type=F32)
        out[:, cols] = (res[:, cols].astype(F32) + gathered).astype(BF16)


def by_offset(array, n, device):
    axes = n.bit_length() - 1
    cut = array.reshape((2,) * axes + array.shape[1:])
    for axis in range(axes):
        bit = (device // (n >> (axis + 1))) % 2
        cut = jnp.where(bit == 1, jnp.flip(cut, axis), cut)
    return cut.reshape(array.shape)


def shards(
    queries, keys_in, values, stream, log_decay, token_index, route_weight, moe_gain,
    out_weight, gate_weight, up_weight, down_weight,
):
    n = lax.axis_size("seq")
    device = lax.axis_index("seq")
    length, width = queries.shape
    heads = log_decay.shape[1]
    size = width // heads
    half = heads // 2
    bits = n.bit_length() - 2
    inner = gate_weight.shape[2]
    vmem = pl.BlockSpec(memory_space=pltpu.VMEM)
    anywhere = pl.BlockSpec(memory_space=pl.ANY)
    dma = pltpu.SemaphoreType.DMA
    rows_of = jax.ShapeDtypeStruct((length, width), BF16)

    residual, mixed_in = pl.pallas_call(
        functools.partial(attend_kernel, n, heads, size),
        out_shape=(rows_of, rows_of),
        in_specs=[anywhere] * 4 + [vmem] * 3 + [anywhere],
        out_specs=(vmem, vmem),
        scratch_shapes=[
            pltpu.VMEM((length, width), BF16),
            pltpu.VMEM((length, width), BF16),
            pltpu.VMEM((length, width), BF16),
            pltpu.VMEM((length, width), BF16),
            pltpu.VMEM((width, width), BF16),
            pltpu.VMEM((length, width), F32),
            pltpu.VMEM((length, width), BF16),
            pltpu.VMEM((length, heads), F32),
            pltpu.VMEM((heads, length), F32),
            pltpu.VMEM((heads, size, size), F32),
            pltpu.VMEM((heads, size, size), BF16),
            pltpu.VMEM((heads, size, size), BF16),
            pltpu.VMEM((half, size, size), F32),
            pltpu.VMEM((half, size, size), F32),
            pltpu.VMEM((bits, half, size, size), BF16),
            pltpu.VMEM((bits, half, size, size), BF16),
            pltpu.VMEM((half, size, size), BF16),
            pltpu.VMEM((half, size, size), BF16),
            pltpu.VMEM((heads, size, size), BF16),
            pltpu.VMEM((n, heads, size), F32),
            pltpu.VMEM((3, heads, size), F32),
            dma((5,)),
            dma((max(n, 13),)),
            dma((max(n, 13),)),
            dma((n,)),
            dma((n,)),
            dma((bits + 2,)),
            dma((bits + 2,)),
        ],
        compiler_params=pltpu.CompilerParams(
            collective_id=0, has_side_effects=True, vmem_limit_bytes=48 * 2**20
        ),
        cost_estimate=pl.CostEstimate(
            flops=2 * length * width * width, bytes_accessed=12 * length * width, transcendentals=0
        ),
        name="attend",
    )(
        queries, keys_in, values, stream, log_decay, log_decay.T, moe_gain[None, :], out_weight
    )

    chosen = token_index.shape[1]
    slots = -(-chosen // 16) * 16
    fill = ((0, 0), (0, slots - chosen))
    places = jnp.pad(token_index - device * length, fill, constant_values=-1)
    places = by_offset(places, n, device)
    route = by_offset(jnp.pad(route_weight, fill), n, device).reshape(1, n * slots)

    return pl.pallas_call(
        functools.partial(expert_kernel, n, slots),
        out_shape=rows_of,
        in_specs=[vmem] * 5 + [anywhere] * 3,
        out_specs=vmem,
        scratch_shapes=[
            pltpu.VMEM((width, inner), BF16),
            pltpu.VMEM((width, inner), BF16),
            pltpu.VMEM((inner, width), BF16),
            pltpu.VMEM((n * slots, width), BF16),
            pltpu.VMEM((n * slots, width), BF16),
            pltpu.VMEM((n * slots, inner), BF16),
            pltpu.VMEM((n * slots, width), BF16),
            pltpu.VMEM((n * slots, width), BF16),
            dma((3,)),
            dma((n,)),
            dma((n,)),
            dma((n,)),
            dma((n,)),
        ],
        compiler_params=pltpu.CompilerParams(
            collective_id=1, has_side_effects=True, vmem_limit_bytes=56 * 2**20
        ),
        cost_estimate=pl.CostEstimate(
            flops=6 * n * slots * width * inner, bytes_accessed=6 * width * inner, transcendentals=0
        ),
        name="experts",
    )(
        mixed_in, residual, places.reshape(n * slots, 1), places.reshape(1, n * slots), route,
        gate_weight[0], up_weight[0], down_weight[0],
    )


def solution(mesh):
    placed = (
        P(("dp", "seq"), None),
        P(("dp", "seq"), None),
        P(("dp", "seq"), None),
        P(("dp", "seq"), None),
        P(("dp", "seq"), None),
        P("dp", "seq"),
        P("dp", "seq"),
        P(),
        P("seq", None),
        P("seq", None, None),
        P("seq", None, None),
        P("seq", None, None),
    )
    return jax.shard_map(
        shards, mesh=mesh, in_specs=placed, out_specs=P(("dp", "seq"), None), check_vma=False
    )
```

```python
import functools

import jax
import jax.numpy as jnp
from jax import lax
from jax.experimental import pallas as pl
from jax.experimental.pallas import tpu as pltpu
from jax.sharding import PartitionSpec as P

MESH = pl.DeviceIdType.MESH
F32, BF16 = jnp.float32, jnp.bfloat16
EXACT = lax.Precision.HIGHEST


def flipped(index, offset):
    bit = 1
    while bit <= offset:
        if offset & bit:
            index = index + bit * (1 - 2 * ((index // bit) % 2))
        bit *= 2
    return index


def remote(src, dst, send, recv, peer):
    return pltpu.make_async_remote_copy(
        src_ref=src, dst_ref=dst, send_sem=send, recv_sem=recv,
        device_id={"seq": peer}, device_id_type=MESH,
    )


def greet(n, me):
    barrier = pltpu.get_barrier_semaphore()
    for offset in range(1, n):
        pl.semaphore_signal(
            barrier, inc=1, device_id={"seq": flipped(me, offset)}, device_id_type=MESH
        )
    pl.semaphore_wait(barrier, n - 1)


def layer_kernel(
    n, heads, size, slots,
    q_h, k_h, v_h, s_h, ldt_h, gain_h, w_h, tok_h, route_h, gate_h, up_h, down_h,
    out,
    q, k, v, stream, ldt, gain, tok, route, gate, up, down,
    weight, att, normed, run, runt,
    state, state_low, state_mate, total, before, give, take, before_low, before_mate,
    incoming, ends, coef,
    arrived, hidden, returned,
    load_sem, w_send, w_recv, e_send, e_recv, s_send, s_recv,
    a_send, a_recv, b_send, b_recv, o_sem,
):
    me = lax.axis_index("seq")
    core, chip = me % 2, me // 2
    mate = flipped(me, 1)
    length, width = q.shape
    rows = w_h.shape[0]
    half = heads // 2
    low = rows // 2
    bits = n.bit_length() - 2
    scaling = size ** (-0.5)

    own_rows = pl.ds(pl.multiple_of(me * rows, rows), rows)
    loads = [
        pltpu.make_async_copy(src, dst, load_sem.at[i])
        for i, (src, dst) in enumerate((
            (k_h, k), (v_h, v), (q_h, q), (s_h, stream), (w_h, weight.at[own_rows]),
            (ldt_h, ldt), (gain_h, gain), (tok_h, tok), (route_h, route),
            (gate_h, gate), (up_h, up), (down_h, down),
        ))
    ]
    for i in (5, 0, 1, 2, 4, 3, 6, 7, 8):
        loads[i].start()
    greet(n, me)

    def part(offset, piece):
        start = flipped(me, offset) * rows
        if piece == 0:
            return pl.ds(pl.multiple_of(start, low), low)
        if piece == 1:
            return pl.ds(pl.multiple_of(start + low, low), low)
        return pl.ds(pl.multiple_of(start, rows), rows)

    def own(piece):
        return w_h.at[pl.ds(piece * low, low)] if piece < 2 else w_h

    def spread(slot, src, where, offset):
        return remote(src, weight.at[where], w_send.at[slot], w_recv.at[slot], flipped(me, offset))

    square = n == 8
    if square:
        first = [
            spread(0, own(0), part(0, 0), 2),
            spread(1, own(1), part(0, 1), 4),
        ]
        second = [
            spread(2, own(1), part(0, 1), 2),
            spread(3, own(0), part(0, 0), 4),
        ]
        onward = [
            spread(4, weight.at[part(2, 0)], part(2, 0), 4),
            spread(5, weight.at[part(4, 1)], part(4, 1), 2),
        ]
        across_own = [spread(6, own(2), part(0, 2), 1)]
        across = [
            spread(7 + i, weight.at[part(o, p)], part(o, p), 1)
            for i, (o, p) in enumerate(((2, 0), (4, 1), (2, 1), (4, 0), (6, 0), (6, 1)))
        ]
    else:
        others = range(2, n, 2)
        first = [spread(o, own(2), part(0, 2), o) for o in others]
        second, onward = [], []
        across_own = [spread(1, own(2), part(0, 2), 1)]
        across = [spread(o + 1, weight.at[part(o, 2)], part(o, 2), 1) for o in others]
    for copy in first + across_own:
        copy.start()

    wide = lax.broadcasted_iota(jnp.int32, (length, length), 0)
    tall = lax.broadcasted_iota(jnp.int32, (length, length), 1)
    lower = (wide >= tall).astype(F32)
    upper = (wide <= tall).astype(F32)
    loads[5].wait()
    run[...] = lax.dot_general(
        lower, ldt[...], (((1,), (1,)), ((), ())), precision=EXACT, preferred_element_type=F32
    )
    runt[...] = jnp.dot(ldt[...], upper, precision=EXACT, preferred_element_type=F32)
    ends[me] = jnp.dot(
        ldt[...], jnp.ones((length, size), F32), precision=EXACT, preferred_element_type=F32
    )
    tell = [
        remote(ends.at[me], ends.at[me], e_send.at[o], e_recv.at[o], flipped(me, o))
        for o in range(1, n)
    ]
    for copy in tell:
        copy.start()

    def column(h):
        here = lax.broadcasted_iota(jnp.int32, (length, heads), 1) == h
        return jnp.sum(jnp.where(here, run[...], 0.0), axis=1, keepdims=True)

    def lanes_of(h):
        return pl.ds(pl.multiple_of(h * size, size), size)

    chosen = tok.shape[1]

    def flat(source, first, count, otherwise):
        lanes = count * slots
        slot = lax.broadcasted_iota(jnp.int32, (chosen, lanes), 0)
        lane = lax.broadcasted_iota(jnp.int32, (chosen, lanes), 1)
        line = lax.broadcasted_iota(jnp.int32, (n, lanes), 0)
        along = lax.broadcasted_iota(jnp.int32, (n, lanes), 1)
        spot = jnp.zeros((chosen, lanes), F32)
        own_line = jnp.zeros((n, lanes), F32)
        for i in range(count):
            spot = jnp.where(lane == slot + i * slots, 1.0, spot)
            within = (along >= i * slots) & (along < i * slots + chosen)
            own_line = jnp.where(within & (line == flipped(me, first + i)), 1.0, own_line)
        placed = jnp.dot(source, spot, precision=EXACT, preferred_element_type=F32) * own_line
        filled = jnp.sum(own_line, axis=0, keepdims=True)
        return jnp.sum(placed, axis=0, keepdims=True) + otherwise * (1.0 - filled)

    loads[0].wait()
    loads[1].wait()

    @pl.loop(0, heads)
    def _(h):
        shrink = jnp.exp(ends[me, pl.ds(h, 1), :] - column(h))
        scaled = (k[:, lanes_of(h)].astype(F32) * shrink).astype(BF16)
        new = lax.dot_general(
            scaled, v[:, lanes_of(h)], (((0,), (0,)), ((), ())), preferred_element_type=F32
        )
        state[h] = new
        state_low[h] = new.astype(BF16)

    swap = remote(state_low, state_mate, s_send.at[0], s_recv.at[0], mate)
    swap.start()
    for copy in tell:
        copy.wait()
    swap.wait()

    first_end, last_end = ends[2 * chip], ends[2 * chip + 1]
    coef[0] = jnp.exp(last_end)

    @pl.loop(0, half)
    def _(j):
        h = core * half + j
        mine, theirs = state[h], state_mate[h].astype(F32)
        early = jnp.where(core == 0, mine, theirs)
        late = jnp.where(core == 0, theirs, mine)
        both = early * coef[0, pl.ds(h, 1), :] + late
        total[j] = both
        give[0, j] = both.astype(BF16)
        before[j] = jnp.zeros_like(both)

    def exchange(b):
        return remote(
            give.at[b], take.at[b], s_send.at[b + 1], s_recv.at[b + 1], flipped(me, 2 << b)
        )

    def bit_of(b):
        return (me // (2 << b)) % 2

    def send_state(b):
        if b < bits - 1:
            exchange(b).start()
        else:

            @pl.when(bit_of(b) == 0)
            def _():
                exchange(b).start()

    send_state(0)
    for copy in second + loads[9:]:
        copy.start()
    loads[2].wait()

    def attend(h):
        grown, across_row = column(h), runt[pl.ds(h, 1), :]
        strips = []
        for first in range(0, length, size):
            keys = k[pl.ds(first, size), lanes_of(h)]
            weights = lax.dot_general(
                q[pl.ds(first, length - first), lanes_of(h)], keys, (((1,), (1,)), ((), ())),
                preferred_element_type=F32,
            ) * scaling
            spacing = grown[first:] - across_row[:, first:first + size]
            strip = weights * jnp.exp(jnp.minimum(spacing, 0.0))
            corner = lax.broadcasted_iota(jnp.int32, (size, size), 0) >= (
                lax.broadcasted_iota(jnp.int32, (size, size), 1)
            )
            strip = [jnp.where(corner, strip[:size], 0.0).astype(BF16), strip[size:].astype(BF16)]
            if first:
                strip.insert(0, jnp.zeros((first, size), BF16))
            strips.append(jnp.concatenate([p for p in strip if p.shape[0]], axis=0))
        att[:, lanes_of(h)] = jnp.dot(
            jnp.concatenate(strips, axis=1), v[:, lanes_of(h)], preferred_element_type=F32
        )

    pl.loop(0, heads)(attend)

    group, ahead = first_end + last_end, jnp.zeros_like(first_end)
    for b in range(bits):
        base = (flipped(me, 2 << b) // (2 << b)) * (2 << b)
        other = ends[base]
        for i in range(1, 2 << b):
            other = other + ends[base + i]
        bit = bit_of(b)
        coef[0] = jnp.exp(ahead)
        coef[1] = jnp.where(bit == 1, jnp.exp(group), 1.0)
        coef[2] = jnp.where(bit == 1, 1.0, jnp.exp(other))
        if b < bits - 1:
            exchange(b).wait()
        else:

            @pl.when(bit == 0)
            def _():
                exchange(b).wait_send()

            @pl.when(bit == 1)
            def _():
                exchange(b).wait_recv()

        @pl.when(bit == 1)
        def _():
            @pl.loop(0, half)
            def _(j):
                h = core * half + j
                before[j] += take[b, j].astype(F32) * coef[0, pl.ds(h, 1), :]

        if b < bits - 1:

            @pl.loop(0, half)
            def _(j):
                h = core * half + j
                both = (
                    take[b, j].astype(F32) * coef[1, pl.ds(h, 1), :]
                    + total[j] * coef[2, pl.ds(h, 1), :]
                )
                total[j] = both
                give[b + 1, j] = both.astype(BF16)

            send_state(b + 1)
        ahead = ahead + jnp.where(bit == 1, other, 0.0)
        group = group + other
        if b == 0 and square:
            first[0].wait_recv()
            onward[0].start()
            across[0].start()
            first[1].wait_recv()
            onward[1].start()
            across[1].start()

    before_low[...] = before[...].astype(BF16)
    trade = remote(before_low, before_mate, s_send.at[bits + 1], s_recv.at[bits + 1], mate)
    trade.start()
    trade.wait()
    coef[0] = jnp.where(core == 1, jnp.exp(first_end), 1.0)

    @pl.loop(0, half)
    def _(j):
        for h, earlier in (
            (core * half + j, before[j]),
            ((1 - core) * half + j, before_mate[j].astype(F32)),
        ):
            mate_part = jnp.where(core == 1, state_mate[h].astype(F32), 0.0)
            incoming[h] = (earlier * coef[0, pl.ds(h, 1), :] + mate_part).astype(BF16)

    @pl.loop(0, heads)
    def _(h):
        grown = jnp.exp(column(h)) * scaling
        scaled = (q[:, lanes_of(h)].astype(F32) * grown).astype(BF16)
        whole = att[:, lanes_of(h)] + jnp.dot(scaled, incoming[h], preferred_element_type=F32)
        mean = jnp.mean(whole * whole, axis=1, keepdims=True)
        normed[:, lanes_of(h)] = (whole * lax.rsqrt(mean + 1e-06)).astype(BF16)

    tile = 512

    def project(offset, fresh):
        start = (flipped(me, offset) // 2) * (2 * rows)
        inner = pl.ds(pl.multiple_of(start, 2 * rows), 2 * rows)

        @pl.loop(0, width // tile)
        def _(i):
            cols = pl.ds(pl.multiple_of(i * tile, tile), tile)
            term = jnp.dot(normed[:, inner], weight[inner, cols], preferred_element_type=F32)
            att[:, cols] = term if fresh else att[:, cols] + term

    loads[4].wait()
    across_own[0].wait()
    project(0, True)
    if square:
        second[0].wait_recv()
        across[2].start()
        second[1].wait_recv()
        across[3].start()
        across[0].wait()
        across[2].wait()
        project(2, False)
        across[1].wait()
        across[3].wait()
        project(4, False)
        onward[0].wait_recv()
        across[4].start()
        onward[1].wait_recv()
        across[5].start()
        loads[3].wait()
        across[4].wait()
        across[5].wait()
        project(6, False)
    else:
        for i, copy in enumerate(first):
            copy.wait()
            across[i].start()
        loads[3].wait()
        for i, offset in enumerate(range(2, n, 2)):
            across[i].wait()
            project(offset, False)

    if square:
        for copy in first + second + onward:
            copy.wait_send()
    res, mix = q, k
    loads[6].wait()
    step = 64

    @pl.loop(0, length // step)
    def _(i):
        at = pl.ds(pl.multiple_of(i * step, step), step)
        kept = (stream[at, :].astype(F32) + att[at, :]).astype(BF16)
        res[at, :] = kept
        kept = kept.astype(F32)
        mean = jnp.mean(kept * kept, axis=1, keepdims=True)
        mix[at, :] = (kept * lax.rsqrt(mean + 1e-06) * gain[...]).astype(BF16)

    inner = gate.shape[1]
    picked = weight.at[pl.ds(0, n * slots)]
    produced = weight.at[pl.ds(n * slots, n * slots)]

    def block(first, count=1):
        return pl.ds(first * slots, count * slots)

    def pick(first, count, into):
        lines = block(first, count)
        lanes = count * slots
        row = flat(tok[...].astype(F32), first, count, -1.0)
        column_of = jnp.broadcast_to(row, (size, lanes)).T
        own_first = me * length
        one_hot = jnp.concatenate([
            jnp.where(
                jnp.abs(
                    column_of
                    - (lax.broadcasted_iota(jnp.int32, (lanes, size), 1) + own_first + at).astype(F32)
                ) < 0.5, 1.0, 0.0,
            ).astype(BF16)
            for at in range(0, length, size)
        ], axis=1)
        tile = 512

        @pl.loop(0, width // tile)
        def _(i):
            cols = pl.ds(pl.multiple_of(i * tile, tile), tile)
            into[lines, cols] = jnp.dot(
                one_hot, mix[:, cols], preferred_element_type=F32
            ).astype(BF16)

    def out_copy(o):
        return remote(
            picked.at[block(o)], arrived.at[block(o)], a_send.at[o], a_recv.at[o], flipped(me, o)
        )

    def back_copy(o):
        return remote(
            produced.at[block(o)], returned.at[block(o)], b_send.at[o], b_recv.at[o],
            flipped(me, o),
        )

    def expert(first, count):
        lines = block(first, count)
        tile = 256

        def upward(cols):
            x = arrived[lines, :]
            a = jnp.dot(x, gate[:, cols], preferred_element_type=F32)
            b = jnp.dot(x, up[:, cols], preferred_element_type=F32)
            hidden[lines, cols] = (a / (1.0 + jnp.exp(-a)) * b).astype(BF16)

        @pl.loop(0, inner // tile)
        def _(i):
            upward(pl.ds(pl.multiple_of(i * tile, tile), tile))

        if inner % tile:
            upward(pl.ds(inner - inner % tile, inner % tile))

        wide = 512

        @pl.loop(0, width // wide)
        def _(i):
            cols = pl.ds(pl.multiple_of(i * wide, wide), wide)
            produced[lines, cols] = jnp.dot(
                hidden[lines, :], down[:, cols], preferred_element_type=F32
            ).astype(BF16)

    near = list(range(2, n - n // 4))
    far = list(range(n - n // 4, n))
    loads[7].wait()
    loads[8].wait()
    pick(2, len(near), picked)
    for o in near:
        out_copy(o).start()
    pick(1, 1, picked)
    out_copy(1).start()
    pick(0, 1, arrived)
    pick(far[0], len(far), picked)
    for copy in loads[9:]:
        copy.wait()
    out_copy(1).wait()
    expert(0, 2)
    back_copy(1).start()
    returned[block(0), :] = produced[block(0), :]
    for o in near:
        out_copy(o).wait_send()
    for o in far:
        out_copy(o).start()
    for o in near:
        out_copy(o).wait_recv()
    expert(2, len(near))
    for o in near:
        back_copy(o).start()
    for o in far:
        out_copy(o).wait()
    expert(far[0], len(far))
    for o in far:
        back_copy(o).start()

    def mixing(first, count):
        lanes = count * slots
        token = flat(tok[...].astype(F32), first, count, -1.0)
        share = flat(route[...], first, count, 0.0)
        line = (lax.broadcasted_iota(jnp.int32, (length, lanes), 0) + me * length).astype(F32)
        return jnp.where(jnp.abs(line - token) < 0.5, share, 0.0).astype(BF16)

    tile = 512
    early, late = mixing(0, far[0]), mixing(far[0], len(far))
    for o in [1] + near:
        back_copy(o).wait()

    @pl.loop(0, width // tile)
    def _(i):
        cols = pl.ds(pl.multiple_of(i * tile, tile), tile)
        gathered = jnp.dot(
            early, returned[block(0, far[0]), cols], preferred_element_type=F32
        )
        att[:, cols] = res[:, cols].astype(F32) + gathered

    for o in far:
        back_copy(o).wait()
    writes = []
    for i in range(width // tile):
        cols = pl.ds(i * tile, tile)
        att[:, cols] += jnp.dot(
            late, returned[block(far[0], len(far)), cols], preferred_element_type=F32
        )
        writes.append(pltpu.make_async_copy(att.at[:, cols], out.at[:, cols], o_sem.at[i]))
        writes[-1].start()
    for copy in writes:
        copy.wait()


def shards(
    queries, keys_in, values, stream, log_decay, token_index, route_weight, moe_gain,
    out_weight, gate_weight, up_weight, down_weight,
):
    n = lax.axis_size("seq")
    device = lax.axis_index("seq")
    length, width = queries.shape
    heads = log_decay.shape[1]
    size = width // heads
    half = heads // 2
    bits = n.bit_length() - 2
    inner = gate_weight.shape[2]
    hbm = pl.BlockSpec(memory_space=pltpu.HBM)
    dma = pltpu.SemaphoreType.DMA
    chosen = token_index.shape[1]
    slots = -(-chosen // 16) * 16

    total = pl.pallas_call(
        functools.partial(layer_kernel, n, heads, size, slots),
        out_shape=jax.ShapeDtypeStruct((length, width), F32),
        in_specs=[hbm] * 12,
        out_specs=hbm,
        scratch_shapes=[
            pltpu.VMEM((length, width), BF16),
            pltpu.VMEM((length, width), BF16),
            pltpu.VMEM((length, width), BF16),
            pltpu.VMEM((length, width), BF16),
            pltpu.VMEM((heads, length), F32),
            pltpu.VMEM((1, width), F32),
            pltpu.VMEM((n, chosen), jnp.int32),
            pltpu.VMEM((n, chosen), F32),
            pltpu.VMEM((width, inner), BF16),
            pltpu.VMEM((width, inner), BF16),
            pltpu.VMEM((inner, width), BF16),
            pltpu.VMEM((width, width), BF16),
            pltpu.VMEM((length, width), F32),
            pltpu.VMEM((length, width), BF16),
            pltpu.VMEM((length, heads), F32),
            pltpu.VMEM((heads, length), F32),
            pltpu.VMEM((heads, size, size), F32),
            pltpu.VMEM((heads, size, size), BF16),
            pltpu.VMEM((heads, size, size), BF16),
            pltpu.VMEM((half, size, size), F32),
            pltpu.VMEM((half, size, size), F32),
            pltpu.VMEM((bits, half, size, size), BF16),
            pltpu.VMEM((bits, half, size, size), BF16),
            pltpu.VMEM((half, size, size), BF16),
            pltpu.VMEM((half, size, size), BF16),
            pltpu.VMEM((heads, size, size), BF16),
            pltpu.VMEM((n, heads, size), F32),
            pltpu.VMEM((3, heads, size), F32),
            pltpu.VMEM((n * slots, width), BF16),
            pltpu.VMEM((n * slots, inner), BF16),
            pltpu.VMEM((n * slots, width), BF16),
            dma((12,)),
            dma((max(n, 13),)),
            dma((max(n, 13),)),
            dma((n,)),
            dma((n,)),
            dma((bits + 2,)),
            dma((bits + 2,)),
            dma((n,)),
            dma((n,)),
            dma((n,)),
            dma((n,)),
            dma((width // 512,)),
        ],
        compiler_params=pltpu.CompilerParams(
            collective_id=0, has_side_effects=True, vmem_limit_bytes=62 * 2**20
        ),
        cost_estimate=pl.CostEstimate(
            flops=2 * length * width * width + 6 * n * slots * width * inner,
            bytes_accessed=6 * width * inner + 14 * length * width, transcendentals=0,
        ),
        name="layer",
    )(
        queries, keys_in, values, stream, log_decay.T, moe_gain[None, :], out_weight,
        token_index, route_weight, gate_weight[0], up_weight[0], down_weight[0],
    )
    return total.astype(BF16)


def solution(mesh):
    placed = (
        P(("dp", "seq"), None),
        P(("dp", "seq"), None),
        P(("dp", "seq"), None),
        P(("dp", "seq"), None),
        P(("dp", "seq"), None),
        P("dp", "seq"),
        P("dp", "seq"),
        P(),
        P("seq", None),
        P("seq", None, None),
        P("seq", None, None),
        P("seq", None, None),
    )
    return jax.shard_map(
        shards, mesh=mesh, in_specs=placed, out_specs=P(("dp", "seq"), None), check_vma=False
    )
```

```python
import functools

import jax
import jax.numpy as jnp
from jax import lax
from jax.experimental import pallas as pl
from jax.experimental.pallas import tpu as pltpu
from jax.sharding import PartitionSpec as P

MESH = pl.DeviceIdType.MESH
F32, BF16 = jnp.float32, jnp.bfloat16
EXACT = lax.Precision.HIGHEST


def flipped(index, offset):
    bit = 1
    while bit <= offset:
        if offset & bit:
            index = index + bit * (1 - 2 * ((index // bit) % 2))
        bit *= 2
    return index


def remote(src, dst, send, recv, peer):
    return pltpu.make_async_remote_copy(
        src_ref=src, dst_ref=dst, send_sem=send, recv_sem=recv,
        device_id={"seq": peer}, device_id_type=MESH,
    )


def greet(n, me, plane=None):
    barrier = pltpu.get_barrier_semaphore()
    for offset in range(1, n):
        pl.semaphore_signal(
            barrier, inc=1, device_id={"seq": flipped(me, offset)}, device_id_type=MESH
        )
    if plane is not None:
        pl.semaphore_signal(barrier, inc=1, device_id={"dp": plane}, device_id_type=MESH)
    pl.semaphore_wait(barrier, n - 1 if plane is None else n)


def layer_kernel(
    n, heads, size, slots,
    q_h, k_h, v_h, s_h, ldt_h, gain_h, w_h, tok_h, route_h, gate_h, up_h, down_h,
    out,
    q, k, v, stream, ldt, gain, tok, route, gate, up, down,
    weight, att, normed, run, runt,
    state, state_low, state_mate, total, before, give, take, before_low, before_mate,
    incoming, ends, coef,
    arrived, hidden, returned,
    load_sem, w_send, w_recv, e_send, e_recv, s_send, s_recv,
    a_send, a_recv, b_send, b_recv, o_sem,
):
    me = lax.axis_index("seq")
    core, chip = me % 2, me // 2
    mate = flipped(me, 1)
    length, width = q.shape
    rows = w_h.shape[0]
    half = heads // 2
    bits = n.bit_length() - 2
    scaling = size ** (-0.5)

    own_rows = pl.ds(pl.multiple_of(me * rows, rows), rows)
    loads = [
        pltpu.make_async_copy(src, dst, load_sem.at[i])
        for i, (src, dst) in enumerate((
            (k_h, k), (v_h, v), (q_h, q), (s_h, stream), (w_h, weight.at[own_rows]),
            (ldt_h, ldt), (gain_h, gain), (tok_h, tok), (route_h, route),
            (gate_h, gate), (up_h, up), (down_h, down),
        ))
    ]
    for i in (4, 5, 0, 1, 2, 3, 6, 7, 8):
        loads[i].start()
    square = n == 8 and lax.axis_size("dp") % 2 == 0
    plane = flipped(lax.axis_index("dp"), 1)
    odd = lax.axis_index("dp") % 2
    greet(n, me, plane if square else None)

    pieces = 8
    some = rows // pieces

    def strip(device, piece=None):
        if piece is None:
            return pl.ds(pl.multiple_of(device * rows, rows), rows)
        return pl.ds(pl.multiple_of(device * rows + piece * some, some), some)

    def spread(slot, where, axis, peer):
        return pltpu.make_async_remote_copy(
            src_ref=weight.at[where], dst_ref=weight.at[where],
            send_sem=w_send.at[slot], recv_sem=w_recv.at[slot],
            device_id={axis: peer}, device_id_type=MESH,
        )

    if square:
        beside = flipped(me, 4)
        sent_x = me + odd * (beside - me)
        from_x = flipped(sent_x, 2)
        from_z = flipped(from_x, 4)
        along_y = [spread(i, strip(me, i), "seq", beside) for i in range(pieces)]
        along_x = [
            spread(pieces + i, strip(sent_x, i), "seq", flipped(me, 2)) for i in range(pieces)
        ]
        along_z = [spread(2 * pieces + i, strip(from_x, i), "dp", plane) for i in range(pieces)]
        share_own = spread(6 * pieces, strip(me), "seq", mate)
        share_y, share_x, share_z = [
            [spread((3 + j) * pieces + i, strip(kind, i), "seq", mate) for i in range(pieces)]
            for j, kind in enumerate((beside, from_x, from_z))
        ]
    else:
        others = range(2, n, 2)
        direct = [spread(o, strip(me), "seq", flipped(me, o)) for o in others]
        share_own = spread(1, strip(me), "seq", mate)
        share = [spread(o + 1, strip(flipped(me, o)), "seq", mate) for o in others]

    def begin(first, last):
        if not square:
            return
        for i in range(first, last):
            along_y[i].start()

        @pl.when(odd == 0)
        def _():
            for i in range(first, last):
                along_x[i].start()

    def relay(turn):
        if not square:
            return
        if turn < pieces:
            along_y[turn].wait_recv()

            @pl.when(odd == 1)
            def _():
                along_x[turn].start()

            share_y[turn].start()
        if 0 <= turn - 1 < pieces:
            along_x[turn - 1].wait_recv()
            along_z[turn - 1].start()
            share_x[turn - 1].start()
        if 0 <= turn - 2 < pieces:
            along_z[turn - 2].wait_recv()
            share_z[turn - 2].start()

    loads[4].wait()
    begin(0, 3)
    share_own.start()
    if not square:
        for copy in direct:
            copy.start()

    wide = lax.broadcasted_iota(jnp.int32, (length, length), 0)
    tall = lax.broadcasted_iota(jnp.int32, (length, length), 1)
    lower = (wide >= tall).astype(F32)
    upper = (wide <= tall).astype(F32)
    loads[5].wait()
    run[...] = lax.dot_general(
        lower, ldt[...], (((1,), (1,)), ((), ())), precision=EXACT, preferred_element_type=F32
    )
    runt[...] = jnp.dot(ldt[...], upper, precision=EXACT, preferred_element_type=F32)
    ends[me] = jnp.dot(
        ldt[...], jnp.ones((length, size), F32), precision=EXACT, preferred_element_type=F32
    )
    tell = [
        remote(ends.at[me], ends.at[me], e_send.at[o], e_recv.at[o], flipped(me, o))
        for o in range(1, n)
    ]
    for copy in tell:
        copy.start()

    def column(h):
        here = lax.broadcasted_iota(jnp.int32, (length, heads), 1) == h
        return jnp.sum(jnp.where(here, run[...], 0.0), axis=1, keepdims=True)

    def lanes_of(h):
        return pl.ds(pl.multiple_of(h * size, size), size)

    chosen = tok.shape[1]

    def flat(source, first, count, otherwise):
        lanes = count * slots
        slot = lax.broadcasted_iota(jnp.int32, (chosen, lanes), 0)
        lane = lax.broadcasted_iota(jnp.int32, (chosen, lanes), 1)
        line = lax.broadcasted_iota(jnp.int32, (n, lanes), 0)
        along = lax.broadcasted_iota(jnp.int32, (n, lanes), 1)
        spot = jnp.zeros((chosen, lanes), F32)
        own_line = jnp.zeros((n, lanes), F32)
        for i in range(count):
            spot = jnp.where(lane == slot + i * slots, 1.0, spot)
            within = (along >= i * slots) & (along < i * slots + chosen)
            own_line = jnp.where(within & (line == flipped(me, first + i)), 1.0, own_line)
        placed = jnp.dot(source, spot, precision=EXACT, preferred_element_type=F32) * own_line
        filled = jnp.sum(own_line, axis=0, keepdims=True)
        return jnp.sum(placed, axis=0, keepdims=True) + otherwise * (1.0 - filled)

    loads[0].wait()
    loads[1].wait()

    @pl.loop(0, heads)
    def _(h):
        shrink = jnp.exp(ends[me, pl.ds(h, 1), :] - column(h))
        scaled = (k[:, lanes_of(h)].astype(F32) * shrink).astype(BF16)
        new = lax.dot_general(
            scaled, v[:, lanes_of(h)], (((0,), (0,)), ((), ())), preferred_element_type=F32
        )
        state[h] = new
        state_low[h] = new.astype(BF16)

    swap = remote(state_low, state_mate, s_send.at[0], s_recv.at[0], mate)
    swap.start()
    for copy in tell:
        copy.wait()
    swap.wait()

    first_end, last_end = ends[2 * chip], ends[2 * chip + 1]
    coef[0] = jnp.exp(last_end)

    @pl.loop(0, half)
    def _(j):
        h = core * half + j
        mine, theirs = state[h], state_mate[h].astype(F32)
        early = jnp.where(core == 0, mine, theirs)
        late = jnp.where(core == 0, theirs, mine)
        both = early * coef[0, pl.ds(h, 1), :] + late
        total[j] = both
        give[0, j] = both.astype(BF16)
        before[j] = jnp.zeros_like(both)

    def exchange(b):
        return remote(
            give.at[b], take.at[b], s_send.at[b + 1], s_recv.at[b + 1], flipped(me, 2 << b)
        )

    def bit_of(b):
        return (me // (2 << b)) % 2

    def send_state(b):
        if b < bits - 1:
            exchange(b).start()
        else:

            @pl.when(bit_of(b) == 0)
            def _():
                exchange(b).start()

    send_state(0)
    begin(3, pieces)
    for copy in loads[9:]:
        copy.start()
    loads[2].wait()

    def attend(h):
        grown, across_row = column(h), runt[pl.ds(h, 1), :]
        strips = []
        for first in range(0, length, size):
            keys = k[pl.ds(first, size), lanes_of(h)]
            weights = lax.dot_general(
                q[pl.ds(first, length - first), lanes_of(h)], keys, (((1,), (1,)), ((), ())),
                preferred_element_type=F32,
            ) * scaling
            spacing = grown[first:] - across_row[:, first:first + size]
            strip = weights * jnp.exp(jnp.minimum(spacing, 0.0))
            corner = lax.broadcasted_iota(jnp.int32, (size, size), 0) >= (
                lax.broadcasted_iota(jnp.int32, (size, size), 1)
            )
            strip = [jnp.where(corner, strip[:size], 0.0).astype(BF16), strip[size:].astype(BF16)]
            if first:
                strip.insert(0, jnp.zeros((first, size), BF16))
            strips.append(jnp.concatenate([p for p in strip if p.shape[0]], axis=0))
        att[:, lanes_of(h)] = jnp.dot(
            jnp.concatenate(strips, axis=1), v[:, lanes_of(h)], preferred_element_type=F32
        )

    quarter = heads // 4
    pl.loop(0, quarter)(attend)
    relay(0)
    pl.loop(quarter, 2 * quarter)(attend)
    relay(1)

    group, ahead = first_end + last_end, jnp.zeros_like(first_end)
    for b in range(bits):
        base = (flipped(me, 2 << b) // (2 << b)) * (2 << b)
        other = ends[base]
        for i in range(1, 2 << b):
            other = other + ends[base + i]
        bit = bit_of(b)
        coef[0] = jnp.exp(ahead)
        coef[1] = jnp.where(bit == 1, jnp.exp(group), 1.0)
        coef[2] = jnp.where(bit == 1, 1.0, jnp.exp(other))
        if b < bits - 1:
            exchange(b).wait()
        else:

            @pl.when(bit == 0)
            def _():
                exchange(b).wait_send()

            @pl.when(bit == 1)
            def _():
                exchange(b).wait_recv()

        @pl.when(bit == 1)
        def _():
            @pl.loop(0, half)
            def _(j):
                h = core * half + j
                before[j] += take[b, j].astype(F32) * coef[0, pl.ds(h, 1), :]

        if b < bits - 1:

            @pl.loop(0, half)
            def _(j):
                h = core * half + j
                both = (
                    take[b, j].astype(F32) * coef[1, pl.ds(h, 1), :]
                    + total[j] * coef[2, pl.ds(h, 1), :]
                )
                total[j] = both
                give[b + 1, j] = both.astype(BF16)

            send_state(b + 1)
        ahead = ahead + jnp.where(bit == 1, other, 0.0)
        group = group + other
        if b == 0:
            relay(2)
            pl.loop(2 * quarter, 3 * quarter)(attend)
            relay(3)
            pl.loop(3 * quarter, heads)(attend)
            relay(4)

    before_low[...] = before[...].astype(BF16)
    trade = remote(before_low, before_mate, s_send.at[bits + 1], s_recv.at[bits + 1], mate)
    trade.start()
    trade.wait()
    coef[0] = jnp.where(core == 1, jnp.exp(first_end), 1.0)

    @pl.loop(0, half)
    def _(j):
        for h, earlier in (
            (core * half + j, before[j]),
            ((1 - core) * half + j, before_mate[j].astype(F32)),
        ):
            mate_part = jnp.where(core == 1, state_mate[h].astype(F32), 0.0)
            incoming[h] = (earlier * coef[0, pl.ds(h, 1), :] + mate_part).astype(BF16)

    def finish(h):
        grown = jnp.exp(column(h)) * scaling
        scaled = (q[:, lanes_of(h)].astype(F32) * grown).astype(BF16)
        whole = att[:, lanes_of(h)] + jnp.dot(scaled, incoming[h], preferred_element_type=F32)
        mean = jnp.mean(whole * whole, axis=1, keepdims=True)
        normed[:, lanes_of(h)] = (whole * lax.rsqrt(mean + 1e-06)).astype(BF16)

    pl.loop(0, heads // 2)(finish)
    relay(5)
    pl.loop(heads // 2, heads)(finish)
    relay(6)
    tile = 512

    def project(device, fresh=False):
        inner = pl.ds(pl.multiple_of((device // 2) * (2 * rows), 2 * rows), 2 * rows)

        @pl.loop(0, width // tile)
        def _(i):
            cols = pl.ds(pl.multiple_of(i * tile, tile), tile)
            term = jnp.dot(normed[:, inner], weight[inner, cols], preferred_element_type=F32)
            att[:, cols] = term if fresh else att[:, cols] + term

    share_own.wait()
    project(me, True)
    if square:
        relay(pieces - 1)
        for copy in share_y:
            copy.wait()
        project(beside)
        relay(pieces)
        for copy in share_x:
            copy.wait()
        project(from_x)
        relay(pieces + 1)
        loads[3].wait()
        for copy in share_z:
            copy.wait()
        project(from_z)
        for copy in along_y + along_x + along_z:
            copy.wait_send()
    else:
        for i, copy in enumerate(direct):
            copy.wait()
            share[i].start()
        loads[3].wait()
        for i, o in enumerate(range(2, n, 2)):
            share[i].wait()
            project(flipped(me, o))
    res, mix = q, k
    loads[6].wait()
    step = 64

    @pl.loop(0, length // step)
    def _(i):
        at = pl.ds(pl.multiple_of(i * step, step), step)
        kept = (stream[at, :].astype(F32) + att[at, :]).astype(BF16)
        res[at, :] = kept
        kept = kept.astype(F32)
        mean = jnp.mean(kept * kept, axis=1, keepdims=True)
        mix[at, :] = (kept * lax.rsqrt(mean + 1e-06) * gain[...]).astype(BF16)

    inner = gate.shape[1]
    picked = weight.at[pl.ds(0, n * slots)]
    produced = weight.at[pl.ds(n * slots, n * slots)]

    def block(first, count=1):
        return pl.ds(first * slots, count * slots)

    def pick(first, count, into):
        lines = block(first, count)
        lanes = count * slots
        row = flat(tok[...].astype(F32), first, count, -1.0)
        column_of = jnp.broadcast_to(row, (size, lanes)).T
        own_first = me * length
        one_hot = jnp.concatenate([
            jnp.where(
                jnp.abs(
                    column_of
                    - (lax.broadcasted_iota(jnp.int32, (lanes, size), 1) + own_first + at).astype(F32)
                ) < 0.5, 1.0, 0.0,
            ).astype(BF16)
            for at in range(0, length, size)
        ], axis=1)
        tile = 512

        @pl.loop(0, width // tile)
        def _(i):
            cols = pl.ds(pl.multiple_of(i * tile, tile), tile)
            into[lines, cols] = jnp.dot(
                one_hot, mix[:, cols], preferred_element_type=F32
            ).astype(BF16)

    def out_copy(o):
        return remote(
            picked.at[block(o)], arrived.at[block(o)], a_send.at[o], a_recv.at[o], flipped(me, o)
        )

    def back_copy(o):
        return remote(
            produced.at[block(o)], returned.at[block(o)], b_send.at[o], b_recv.at[o],
            flipped(me, o),
        )

    def expert(first, count):
        lines = block(first, count)
        tile = 256

        def upward(cols):
            x = arrived[lines, :]
            a = jnp.dot(x, gate[:, cols], preferred_element_type=F32)
            b = jnp.dot(x, up[:, cols], preferred_element_type=F32)
            hidden[lines, cols] = (a / (1.0 + jnp.exp(-a)) * b).astype(BF16)

        @pl.loop(0, inner // tile)
        def _(i):
            upward(pl.ds(pl.multiple_of(i * tile, tile), tile))

        if inner % tile:
            upward(pl.ds(inner - inner % tile, inner % tile))

        wide = 512

        @pl.loop(0, width // wide)
        def _(i):
            cols = pl.ds(pl.multiple_of(i * wide, wide), wide)
            produced[lines, cols] = jnp.dot(
                hidden[lines, :], down[:, cols], preferred_element_type=F32
            ).astype(BF16)

    near = list(range(2, n - n // 4))
    far = list(range(n - n // 4, n))
    loads[7].wait()
    loads[8].wait()
    pick(2, len(near), picked)
    for o in near:
        out_copy(o).start()
    pick(1, 1, picked)
    out_copy(1).start()
    pick(0, 1, arrived)
    pick(far[0], len(far), picked)
    for copy in loads[9:]:
        copy.wait()
    out_copy(1).wait()
    expert(0, 2)
    back_copy(1).start()
    returned[block(0), :] = produced[block(0), :]
    for o in near:
        out_copy(o).wait_send()
    for o in far:
        out_copy(o).start()
    for o in near:
        out_copy(o).wait_recv()
    expert(2, len(near))
    for o in near:
        back_copy(o).start()
    for o in far:
        out_copy(o).wait()
    expert(far[0], len(far))
    for o in far:
        back_copy(o).start()

    def mixing(first, count):
        lanes = count * slots
        token = flat(tok[...].astype(F32), first, count, -1.0)
        share = flat(route[...], first, count, 0.0)
        line = (lax.broadcasted_iota(jnp.int32, (length, lanes), 0) + me * length).astype(F32)
        return jnp.where(jnp.abs(line - token) < 0.5, share, 0.0).astype(BF16)

    tile = 512
    early, late = mixing(0, far[0]), mixing(far[0], len(far))
    for o in [1] + near:
        back_copy(o).wait()

    @pl.loop(0, width // tile)
    def _(i):
        cols = pl.ds(pl.multiple_of(i * tile, tile), tile)
        gathered = jnp.dot(
            early, returned[block(0, far[0]), cols], preferred_element_type=F32
        )
        att[:, cols] = res[:, cols].astype(F32) + gathered

    for o in far:
        back_copy(o).wait()
    writes = []
    for i in range(width // tile):
        cols = pl.ds(i * tile, tile)
        gathered = jnp.dot(
            late, returned[block(far[0], len(far)), cols], preferred_element_type=F32
        )
        v[:, cols] = (att[:, cols] + gathered).astype(BF16)
        writes.append(pltpu.make_async_copy(v.at[:, cols], out.at[:, cols], o_sem.at[i]))
        writes[-1].start()
    for copy in writes:
        copy.wait()


def shards(
    queries, keys_in, values, stream, log_decay, token_index, route_weight, moe_gain,
    out_weight, gate_weight, up_weight, down_weight,
):
    n = lax.axis_size("seq")
    device = lax.axis_index("seq")
    length, width = queries.shape
    heads = log_decay.shape[1]
    size = width // heads
    half = heads // 2
    bits = n.bit_length() - 2
    inner = gate_weight.shape[2]
    hbm = pl.BlockSpec(memory_space=pltpu.HBM)
    dma = pltpu.SemaphoreType.DMA
    chosen = token_index.shape[1]
    slots = -(-chosen // 16) * 16

    return pl.pallas_call(
        functools.partial(layer_kernel, n, heads, size, slots),
        out_shape=jax.ShapeDtypeStruct((length, width), BF16),
        in_specs=[hbm] * 12,
        out_specs=hbm,
        scratch_shapes=[
            pltpu.VMEM((length, width), BF16),
            pltpu.VMEM((length, width), BF16),
            pltpu.VMEM((length, width), BF16),
            pltpu.VMEM((length, width), BF16),
            pltpu.VMEM((heads, length), F32),
            pltpu.VMEM((1, width), F32),
            pltpu.VMEM((n, chosen), jnp.int32),
            pltpu.VMEM((n, chosen), F32),
            pltpu.VMEM((width, inner), BF16),
            pltpu.VMEM((width, inner), BF16),
            pltpu.VMEM((inner, width), BF16),
            pltpu.VMEM((width, width), BF16),
            pltpu.VMEM((length, width), F32),
            pltpu.VMEM((length, width), BF16),
            pltpu.VMEM((length, heads), F32),
            pltpu.VMEM((heads, length), F32),
            pltpu.VMEM((heads, size, size), F32),
            pltpu.VMEM((heads, size, size), BF16),
            pltpu.VMEM((heads, size, size), BF16),
            pltpu.VMEM((half, size, size), F32),
            pltpu.VMEM((half, size, size), F32),
            pltpu.VMEM((bits, half, size, size), BF16),
            pltpu.VMEM((bits, half, size, size), BF16),
            pltpu.VMEM((half, size, size), BF16),
            pltpu.VMEM((half, size, size), BF16),
            pltpu.VMEM((heads, size, size), BF16),
            pltpu.VMEM((n, heads, size), F32),
            pltpu.VMEM((3, heads, size), F32),
            pltpu.VMEM((n * slots, width), BF16),
            pltpu.VMEM((n * slots, inner), BF16),
            pltpu.VMEM((n * slots, width), BF16),
            dma((12,)),
            dma((max(n, 49),)),
            dma((max(n, 49),)),
            dma((n,)),
            dma((n,)),
            dma((bits + 2,)),
            dma((bits + 2,)),
            dma((n,)),
            dma((n,)),
            dma((n,)),
            dma((n,)),
            dma((width // 512,)),
        ],
        compiler_params=pltpu.CompilerParams(
            collective_id=0, has_side_effects=True, vmem_limit_bytes=62 * 2**20
        ),
        cost_estimate=pl.CostEstimate(
            flops=2 * length * width * width + 6 * n * slots * width * inner,
            bytes_accessed=6 * width * inner + 14 * length * width, transcendentals=0,
        ),
        name="layer",
    )(
        queries, keys_in, values, stream, log_decay.T, moe_gain[None, :], out_weight,
        token_index, route_weight, gate_weight[0], up_weight[0], down_weight[0],
    )


def solution(mesh):
    placed = (
        P(("dp", "seq"), None),
        P(("dp", "seq"), None),
        P(("dp", "seq"), None),
        P(("dp", "seq"), None),
        P(("dp", "seq"), None),
        P("dp", "seq"),
        P("dp", "seq"),
        P(),
        P("seq", None),
        P("seq", None, None),
        P("seq", None, None),
        P("seq", None, None),
    )
    return jax.shard_map(
        shards, mesh=mesh, in_specs=placed, out_specs=P(("dp", "seq"), None), check_vma=False
    )
```

```python
import functools

import jax
import jax.numpy as jnp
from jax import lax
from jax.experimental import pallas as pl
from jax.experimental.pallas import tpu as pltpu
from jax.sharding import PartitionSpec as P

MESH = pl.DeviceIdType.MESH
F32, BF16 = jnp.float32, jnp.bfloat16
EXACT = lax.Precision.HIGHEST


def flipped(index, offset):
    bit = 1
    while bit <= offset:
        if offset & bit:
            index = index + bit * (1 - 2 * ((index // bit) % 2))
        bit *= 2
    return index


def remote(src, dst, send, recv, peer):
    return pltpu.make_async_remote_copy(
        src_ref=src, dst_ref=dst, send_sem=send, recv_sem=recv,
        device_id={"seq": peer}, device_id_type=MESH,
    )


def greet(n, me):
    barrier = pltpu.get_barrier_semaphore()
    for offset in range(1, n):
        pl.semaphore_signal(
            barrier, inc=1, device_id={"seq": flipped(me, offset)}, device_id_type=MESH
        )
    pl.semaphore_wait(barrier, n - 1)


def layer_kernel(
    n, heads, size, slots,
    q_h, k_h, v_h, s_h, ldt_h, gain_h, w_h, tok_h, route_h, gate_h, up_h, down_h,
    out,
    q, k, v, stream, ldt, gain, tok, route, gate, up, down,
    weight, att, normed, run, runt,
    state, state_low, state_mate, total, before, give, take, before_low, before_mate,
    incoming, ends, coef,
    arrived, hidden, returned,
    load_sem, w_send, w_recv, e_send, e_recv, s_send, s_recv,
    a_send, a_recv, b_send, b_recv, o_sem,
):
    me = lax.axis_index("seq")
    core, chip = me % 2, me // 2
    mate = flipped(me, 1)
    length, width = q.shape
    rows = w_h.shape[0]
    half = heads // 2
    low = rows // 2
    bits = n.bit_length() - 2
    scaling = size ** (-0.5)

    own_rows = pl.ds(pl.multiple_of(me * rows, rows), rows)
    loads = [
        pltpu.make_async_copy(src, dst, load_sem.at[i])
        for i, (src, dst) in enumerate((
            (k_h, k), (v_h, v), (q_h, q), (s_h, stream), (w_h, weight.at[own_rows]),
            (ldt_h, ldt), (gain_h, gain), (tok_h, tok), (route_h, route),
            (gate_h, gate), (up_h, up), (down_h, down),
        ))
    ]
    for i in (5, 0, 1, 2, 4, 3, 6, 7, 8):
        loads[i].start()
    greet(n, me)

    def part(offset, piece):
        start = flipped(me, offset) * rows
        if piece == 0:
            return pl.ds(pl.multiple_of(start, low), low)
        if piece == 1:
            return pl.ds(pl.multiple_of(start + low, low), low)
        return pl.ds(pl.multiple_of(start, rows), rows)

    def own(piece):
        return w_h.at[pl.ds(piece * low, low)] if piece < 2 else w_h

    def spread(slot, src, where, offset):
        return remote(src, weight.at[where], w_send.at[slot], w_recv.at[slot], flipped(me, offset))

    square = n == 8
    if square:
        first = [
            spread(0, own(0), part(0, 0), 2),
            spread(1, own(1), part(0, 1), 4),
        ]
        second = [
            spread(2, own(1), part(0, 1), 2),
            spread(3, own(0), part(0, 0), 4),
        ]
        onward = [
            spread(4, weight.at[part(2, 0)], part(2, 0), 4),
            spread(5, weight.at[part(4, 1)], part(4, 1), 2),
        ]
        across_own = [spread(6, own(2), part(0, 2), 1)]
        across = [
            spread(7 + i, weight.at[part(o, p)], part(o, p), 1)
            for i, (o, p) in enumerate(((2, 0), (4, 1), (2, 1), (4, 0), (6, 0), (6, 1)))
        ]
    else:
        others = range(2, n, 2)
        first = [spread(o, own(2), part(0, 2), o) for o in others]
        second, onward = [], []
        across_own = [spread(1, own(2), part(0, 2), 1)]
        across = [spread(o + 1, weight.at[part(o, 2)], part(o, 2), 1) for o in others]
    for copy in first + across_own:
        copy.start()

    wide = lax.broadcasted_iota(jnp.int32, (length, length), 0)
    tall = lax.broadcasted_iota(jnp.int32, (length, length), 1)
    lower = (wide >= tall).astype(F32)
    upper = (wide <= tall).astype(F32)
    loads[5].wait()
    run[...] = lax.dot_general(
        lower, ldt[...], (((1,), (1,)), ((), ())), precision=EXACT, preferred_element_type=F32
    )
    runt[...] = jnp.dot(ldt[...], upper, precision=EXACT, preferred_element_type=F32)
    ends[me] = jnp.dot(
        ldt[...], jnp.ones((length, size), F32), precision=EXACT, preferred_element_type=F32
    )
    tell = [
        remote(ends.at[me], ends.at[me], e_send.at[o], e_recv.at[o], flipped(me, o))
        for o in range(1, n)
    ]
    for copy in tell:
        copy.start()

    def column(h):
        here = lax.broadcasted_iota(jnp.int32, (length, heads), 1) == h
        return jnp.sum(jnp.where(here, run[...], 0.0), axis=1, keepdims=True)

    def lanes_of(h):
        return pl.ds(pl.multiple_of(h * size, size), size)

    chosen = tok.shape[1]

    def flat(source, first, count, otherwise):
        lanes = count * slots
        slot = lax.broadcasted_iota(jnp.int32, (chosen, lanes), 0)
        lane = lax.broadcasted_iota(jnp.int32, (chosen, lanes), 1)
        line = lax.broadcasted_iota(jnp.int32, (n, lanes), 0)
        along = lax.broadcasted_iota(jnp.int32, (n, lanes), 1)
        spot = jnp.zeros((chosen, lanes), F32)
        own_line = jnp.zeros((n, lanes), F32)
        for i in range(count):
            spot = jnp.where(lane == slot + i * slots, 1.0, spot)
            within = (along >= i * slots) & (along < i * slots + chosen)
            own_line = jnp.where(within & (line == flipped(me, first + i)), 1.0, own_line)
        placed = jnp.dot(source, spot, precision=EXACT, preferred_element_type=F32) * own_line
        filled = jnp.sum(own_line, axis=0, keepdims=True)
        return jnp.sum(placed, axis=0, keepdims=True) + otherwise * (1.0 - filled)

    loads[0].wait()
    loads[1].wait()

    @pl.loop(0, heads, unroll=4)
    def _(h):
        shrink = jnp.exp(ends[me, pl.ds(h, 1), :] - column(h))
        scaled = (k[:, lanes_of(h)].astype(F32) * shrink).astype(BF16)
        new = lax.dot_general(
            scaled, v[:, lanes_of(h)], (((0,), (0,)), ((), ())), preferred_element_type=F32
        )
        state[h] = new
        state_low[h] = new.astype(BF16)

    swap = remote(state_low, state_mate, s_send.at[0], s_recv.at[0], mate)
    swap.start()
    for copy in tell:
        copy.wait()
    swap.wait()

    first_end, last_end = ends[2 * chip], ends[2 * chip + 1]
    coef[0] = jnp.exp(last_end)

    @pl.loop(0, half)
    def _(j):
        h = core * half + j
        mine, theirs = state[h], state_mate[h].astype(F32)
        early = jnp.where(core == 0, mine, theirs)
        late = jnp.where(core == 0, theirs, mine)
        both = early * coef[0, pl.ds(h, 1), :] + late
        total[j] = both
        give[0, j] = both.astype(BF16)
        before[j] = jnp.zeros_like(both)

    def exchange(b):
        return remote(
            give.at[b], take.at[b], s_send.at[b + 1], s_recv.at[b + 1], flipped(me, 2 << b)
        )

    def bit_of(b):
        return (me // (2 << b)) % 2

    def send_state(b):
        if b < bits - 1:
            exchange(b).start()
        else:

            @pl.when(bit_of(b) == 0)
            def _():
                exchange(b).start()

    send_state(0)
    for copy in second + loads[9:]:
        copy.start()
    loads[2].wait()

    def attend(h):
        grown, across_row = column(h), runt[pl.ds(h, 1), :]
        strips = []
        for first in range(0, length, size):
            keys = k[pl.ds(first, size), lanes_of(h)]
            weights = lax.dot_general(
                q[pl.ds(first, length - first), lanes_of(h)], keys, (((1,), (1,)), ((), ())),
                preferred_element_type=F32,
            ) * scaling
            spacing = grown[first:] - across_row[:, first:first + size]
            strip = weights * jnp.exp(jnp.minimum(spacing, 0.0))
            corner = lax.broadcasted_iota(jnp.int32, (size, size), 0) >= (
                lax.broadcasted_iota(jnp.int32, (size, size), 1)
            )
            strip = [jnp.where(corner, strip[:size], 0.0).astype(BF16), strip[size:].astype(BF16)]
            if first:
                strip.insert(0, jnp.zeros((first, size), BF16))
            strips.append(jnp.concatenate([p for p in strip if p.shape[0]], axis=0))
        att[:, lanes_of(h)] = jnp.dot(
            jnp.concatenate(strips, axis=1), v[:, lanes_of(h)], preferred_element_type=F32
        )

    pl.loop(0, heads, unroll=2)(attend)

    group, ahead = first_end + last_end, jnp.zeros_like(first_end)
    for b in range(bits):
        base = (flipped(me, 2 << b) // (2 << b)) * (2 << b)
        other = ends[base]
        for i in range(1, 2 << b):
            other = other + ends[base + i]
        bit = bit_of(b)
        coef[0] = jnp.exp(ahead)
        coef[1] = jnp.where(bit == 1, jnp.exp(group), 1.0)
        coef[2] = jnp.where(bit == 1, 1.0, jnp.exp(other))
        if b < bits - 1:
            exchange(b).wait()
        else:

            @pl.when(bit == 0)
            def _():
                exchange(b).wait_send()

            @pl.when(bit == 1)
            def _():
                exchange(b).wait_recv()

        @pl.when(bit == 1)
        def _():
            @pl.loop(0, half)
            def _(j):
                h = core * half + j
                before[j] += take[b, j].astype(F32) * coef[0, pl.ds(h, 1), :]

        if b < bits - 1:

            @pl.loop(0, half)
            def _(j):
                h = core * half + j
                both = (
                    take[b, j].astype(F32) * coef[1, pl.ds(h, 1), :]
                    + total[j] * coef[2, pl.ds(h, 1), :]
                )
                total[j] = both
                give[b + 1, j] = both.astype(BF16)

            send_state(b + 1)
        ahead = ahead + jnp.where(bit == 1, other, 0.0)
        group = group + other
        if b == 0 and square:
            first[0].wait_recv()
            onward[0].start()
            across[0].start()
            first[1].wait_recv()
            onward[1].start()
            across[1].start()

    before_low[...] = before[...].astype(BF16)
    trade = remote(before_low, before_mate, s_send.at[bits + 1], s_recv.at[bits + 1], mate)
    trade.start()
    trade.wait()
    coef[0] = jnp.where(core == 1, jnp.exp(first_end), 1.0)

    @pl.loop(0, half)
    def _(j):
        for h, earlier in (
            (core * half + j, before[j]),
            ((1 - core) * half + j, before_mate[j].astype(F32)),
        ):
            mate_part = jnp.where(core == 1, state_mate[h].astype(F32), 0.0)
            incoming[h] = (earlier * coef[0, pl.ds(h, 1), :] + mate_part).astype(BF16)

    @pl.loop(0, heads, unroll=4)
    def _(h):
        grown = jnp.exp(column(h)) * scaling
        scaled = (q[:, lanes_of(h)].astype(F32) * grown).astype(BF16)
        whole = att[:, lanes_of(h)] + jnp.dot(scaled, incoming[h], preferred_element_type=F32)
        mean = jnp.mean(whole * whole, axis=1, keepdims=True)
        normed[:, lanes_of(h)] = (whole * lax.rsqrt(mean + 1e-06)).astype(BF16)

    tile = 512

    def project(offset, fresh):
        start = (flipped(me, offset) // 2) * (2 * rows)
        inner = pl.ds(pl.multiple_of(start, 2 * rows), 2 * rows)

        @pl.loop(0, width // tile)
        def _(i):
            cols = pl.ds(pl.multiple_of(i * tile, tile), tile)
            term = jnp.dot(normed[:, inner], weight[inner, cols], preferred_element_type=F32)
            att[:, cols] = term if fresh else att[:, cols] + term

    loads[4].wait()
    across_own[0].wait()
    project(0, True)
    if square:
        second[0].wait_recv()
        across[2].start()
        second[1].wait_recv()
        across[3].start()
        across[0].wait()
        across[2].wait()
        project(2, False)
        across[1].wait()
        across[3].wait()
        project(4, False)
        onward[0].wait_recv()
        across[4].start()
        onward[1].wait_recv()
        across[5].start()
        loads[3].wait()
        across[4].wait()
        across[5].wait()
        project(6, False)
    else:
        for i, copy in enumerate(first):
            copy.wait()
            across[i].start()
        loads[3].wait()
        for i, offset in enumerate(range(2, n, 2)):
            across[i].wait()
            project(offset, False)

    if square:
        for copy in first + second + onward:
            copy.wait_send()
    res, mix = q, k
    loads[6].wait()
    step = 64

    @pl.loop(0, length // step)
    def _(i):
        at = pl.ds(pl.multiple_of(i * step, step), step)
        kept = (stream[at, :].astype(F32) + att[at, :]).astype(BF16)
        res[at, :] = kept
        kept = kept.astype(F32)
        mean = jnp.mean(kept * kept, axis=1, keepdims=True)
        mix[at, :] = (kept * lax.rsqrt(mean + 1e-06) * gain[...]).astype(BF16)

    inner = gate.shape[1]
    picked = weight.at[pl.ds(0, n * slots)]
    produced = weight.at[pl.ds(n * slots, n * slots)]

    def block(first, count=1):
        return pl.ds(first * slots, count * slots)

    def pick(first, count, into):
        lines = block(first, count)
        lanes = count * slots
        row = flat(tok[...].astype(F32), first, count, -1.0)
        column_of = jnp.broadcast_to(row, (size, lanes)).T
        own_first = me * length
        one_hot = jnp.concatenate([
            jnp.where(
                jnp.abs(
                    column_of
                    - (lax.broadcasted_iota(jnp.int32, (lanes, size), 1) + own_first + at).astype(F32)
                ) < 0.5, 1.0, 0.0,
            ).astype(BF16)
            for at in range(0, length, size)
        ], axis=1)
        tile = 512

        @pl.loop(0, width // tile)
        def _(i):
            cols = pl.ds(pl.multiple_of(i * tile, tile), tile)
            into[lines, cols] = jnp.dot(
                one_hot, mix[:, cols], preferred_element_type=F32
            ).astype(BF16)

    def out_copy(o):
        return remote(
            picked.at[block(o)], arrived.at[block(o)], a_send.at[o], a_recv.at[o], flipped(me, o)
        )

    def back_copy(o):
        return remote(
            produced.at[block(o)], returned.at[block(o)], b_send.at[o], b_recv.at[o],
            flipped(me, o),
        )

    def expert(first, count):
        lines = block(first, count)
        tile = 256

        def upward(cols):
            x = arrived[lines, :]
            a = jnp.dot(x, gate[:, cols], preferred_element_type=F32)
            b = jnp.dot(x, up[:, cols], preferred_element_type=F32)
            hidden[lines, cols] = (a / (1.0 + jnp.exp(-a)) * b).astype(BF16)

        @pl.loop(0, inner // tile)
        def _(i):
            upward(pl.ds(pl.multiple_of(i * tile, tile), tile))

        if inner % tile:
            upward(pl.ds(inner - inner % tile, inner % tile))

        wide = 512

        @pl.loop(0, width // wide)
        def _(i):
            cols = pl.ds(pl.multiple_of(i * wide, wide), wide)
            produced[lines, cols] = jnp.dot(
                hidden[lines, :], down[:, cols], preferred_element_type=F32
            ).astype(BF16)

    near = list(range(2, n - n // 4))
    far = list(range(n - n // 4, n))
    loads[7].wait()
    loads[8].wait()
    pick(2, len(near), picked)
    for o in near:
        out_copy(o).start()
    pick(1, 1, picked)
    out_copy(1).start()
    pick(0, 1, arrived)
    pick(far[0], len(far), picked)
    for copy in loads[9:]:
        copy.wait()
    out_copy(1).wait()
    expert(0, 2)
    back_copy(1).start()
    returned[block(0), :] = produced[block(0), :]
    for o in near:
        out_copy(o).wait_send()
    for o in far:
        out_copy(o).start()
    for o in near:
        out_copy(o).wait_recv()
    expert(2, len(near))
    for o in near:
        back_copy(o).start()
    for o in far:
        out_copy(o).wait()
    expert(far[0], len(far))
    for o in far:
        back_copy(o).start()

    def mixing(first, count):
        lanes = count * slots
        token = flat(tok[...].astype(F32), first, count, -1.0)
        share = flat(route[...], first, count, 0.0)
        line = (lax.broadcasted_iota(jnp.int32, (length, lanes), 0) + me * length).astype(F32)
        return jnp.where(jnp.abs(line - token) < 0.5, share, 0.0).astype(BF16)

    tile = 512
    early, late = mixing(0, far[0]), mixing(far[0], len(far))
    for o in [1] + near:
        back_copy(o).wait()

    @pl.loop(0, width // tile)
    def _(i):
        cols = pl.ds(pl.multiple_of(i * tile, tile), tile)
        gathered = jnp.dot(
            early, returned[block(0, far[0]), cols], preferred_element_type=F32
        )
        att[:, cols] = res[:, cols].astype(F32) + gathered

    for o in far:
        back_copy(o).wait()
    writes = []
    for i in range(width // tile):
        cols = pl.ds(i * tile, tile)
        gathered = jnp.dot(
            late, returned[block(far[0], len(far)), cols], preferred_element_type=F32
        )
        v[:, cols] = (att[:, cols] + gathered).astype(BF16)
        writes.append(pltpu.make_async_copy(v.at[:, cols], out.at[:, cols], o_sem.at[i]))
        writes[-1].start()
    for copy in writes:
        copy.wait()


def shards(
    queries, keys_in, values, stream, log_decay, token_index, route_weight, moe_gain,
    out_weight, gate_weight, up_weight, down_weight,
):
    n = lax.axis_size("seq")
    device = lax.axis_index("seq")
    length, width = queries.shape
    heads = log_decay.shape[1]
    size = width // heads
    half = heads // 2
    bits = n.bit_length() - 2
    inner = gate_weight.shape[2]
    hbm = pl.BlockSpec(memory_space=pltpu.HBM)
    dma = pltpu.SemaphoreType.DMA
    chosen = token_index.shape[1]
    slots = -(-chosen // 16) * 16

    return pl.pallas_call(
        functools.partial(layer_kernel, n, heads, size, slots),
        out_shape=jax.ShapeDtypeStruct((length, width), BF16),
        in_specs=[hbm] * 12,
        out_specs=hbm,
        scratch_shapes=[
            pltpu.VMEM((length, width), BF16),
            pltpu.VMEM((length, width), BF16),
            pltpu.VMEM((length, width), BF16),
            pltpu.VMEM((length, width), BF16),
            pltpu.VMEM((heads, length), F32),
            pltpu.VMEM((1, width), F32),
            pltpu.VMEM((n, chosen), jnp.int32),
            pltpu.VMEM((n, chosen), F32),
            pltpu.VMEM((width, inner), BF16),
            pltpu.VMEM((width, inner), BF16),
            pltpu.VMEM((inner, width), BF16),
            pltpu.VMEM((width, width), BF16),
            pltpu.VMEM((length, width), F32),
            pltpu.VMEM((length, width), BF16),
            pltpu.VMEM((length, heads), F32),
            pltpu.VMEM((heads, length), F32),
            pltpu.VMEM((heads, size, size), F32),
            pltpu.VMEM((heads, size, size), BF16),
            pltpu.VMEM((heads, size, size), BF16),
            pltpu.VMEM((half, size, size), F32),
            pltpu.VMEM((half, size, size), F32),
            pltpu.VMEM((bits, half, size, size), BF16),
            pltpu.VMEM((bits, half, size, size), BF16),
            pltpu.VMEM((half, size, size), BF16),
            pltpu.VMEM((half, size, size), BF16),
            pltpu.VMEM((heads, size, size), BF16),
            pltpu.VMEM((n, heads, size), F32),
            pltpu.VMEM((3, heads, size), F32),
            pltpu.VMEM((n * slots, width), BF16),
            pltpu.VMEM((n * slots, inner), BF16),
            pltpu.VMEM((n * slots, width), BF16),
            dma((12,)),
            dma((max(n, 13),)),
            dma((max(n, 13),)),
            dma((n,)),
            dma((n,)),
            dma((bits + 2,)),
            dma((bits + 2,)),
            dma((n,)),
            dma((n,)),
            dma((n,)),
            dma((n,)),
            dma((width // 512,)),
        ],
        compiler_params=pltpu.CompilerParams(
            collective_id=0, has_side_effects=True, vmem_limit_bytes=62 * 2**20
        ),
        cost_estimate=pl.CostEstimate(
            flops=2 * length * width * width + 6 * n * slots * width * inner,
            bytes_accessed=6 * width * inner + 14 * length * width, transcendentals=0,
        ),
        name="layer",
    )(
        queries, keys_in, values, stream, log_decay.T, moe_gain[None, :], out_weight,
        token_index, route_weight, gate_weight[0], up_weight[0], down_weight[0],
    )


def solution(mesh):
    placed = (
        P(("dp", "seq"), None),
        P(("dp", "seq"), None),
        P(("dp", "seq"), None),
        P(("dp", "seq"), None),
        P(("dp", "seq"), None),
        P("dp", "seq"),
        P("dp", "seq"),
        P(),
        P("seq", None),
        P("seq", None, None),
        P("seq", None, None),
        P("seq", None, None),
    )
    return jax.shard_map(
        shards, mesh=mesh, in_specs=placed, out_specs=P(("dp", "seq"), None), check_vma=False
    )
```
